32 devices in a mesh: groups: 2 (over x), row: 16 (over z, y, core).
Axes of the slice: x: 2, y: 2, z: 4, core: 2. Of those that a mesh axis runs over, the one named last changes fastest.
Arguments:
- tiles: bfloat16 [2048, 128, 128], P(('groups', 'row')), parts along dimension 0, may hold values from -0.41992188 to 0.41992188
- tile_row: int32 [2048, 1], P(('groups', 'row')), parts along dimension 0, may hold values from 0 to 63; in each aligned block of 64 rows (0 to 63, 64 to 127, ...) at most 2 rows name the same one
- tile_col: int32 [2048, 1], P(('groups', 'row')), parts along dimension 0, may hold values from 0 to 63; in each aligned block of 64 rows (0 to 63, 64 to 127, ...) at most 2 rows name the same one
- tile_aux: int32 [2048], P(('groups', 'row')), parts along dimension 0, may hold values from 0 to 15
- coeffs: bfloat16 [16384, 1024], P(('groups', 'row')), parts along dimension 0, may hold values from -0.5 to 0.5
Outputs:
- pair_ints: float32 [32, 96, 1024], P('groups', None, 'row'), parts along dimension 0
The draws below stay inside these ranges and needn't reach their ends.
There are 2 independent parts, one for each index of `groups`. The reference program is written for one: setup_inputs(seed, part) draws one part's arguments, and reference() takes and returns one part's arrays. A program takes and returns all parts, laid end to end along the dimension named above; each array names one. Nothing has to cross between parts.
Inputs may be any that keep to these rules, and one draw needn't show every extreme that they name: `tile_row`: in the rows of one builder (aligned blocks of 64 tiles) no row block is named by more than 2 tiles; some row block is named by exactly 2. `tile_col`: in the rows of one builder (aligned blocks of 64 tiles) no column block is named by more than 2 tiles; some column block is named by exactly 2.
All inputs are finite; a program needn't handle non-finite values.
Results may differ from the reference program's by a relative error of at most 0.005.
Values may be sent and summed in bfloat16 or wider, within the bound.
A program may use at most 128 MiB of HBM per device.

```python
import math
import jax
import jax.numpy as jnp
import numpy as np
from jax import lax

TILE = 128
NBF = 8192
NOCC = 1024
OI = 96
AUX = 16
NT_DEV = 64
NB = 64
CAP = 2
NTILES = 1024


def place_ends(entries, key, smallest, largest):
    index_at = [jax.random.randint(jax.random.fold_in(key, axis), (), 0, length) for axis, length in enumerate(entries.shape)]
    longest = entries.shape.index(max(entries.shape))
    next_to = index_at[:longest] + [(index_at[longest] + 1) % entries.shape[longest]] + index_at[longest + 1:]
    return entries.at[tuple(index_at)].set(smallest).at[tuple(next_to)].set(largest)


def block_scale(key, shape, split, smallest, high):
    def one(axis_at, blocks):
        steps = jax.random.uniform(jax.random.fold_in(jax.random.fold_in(key, 6), axis_at), (blocks,), jnp.float32, smallest / len(split), high / len(split))
        return jnp.repeat(jnp.exp(steps), shape[axis_at] // blocks).reshape((-1,) + (1,) * (len(shape) - axis_at - 1))

    loudness = one(*split[0])
    for cut in split[1:]:
        loudness = loudness * one(*cut)
    return loudness


def deal_out(stream_key, own, number, rows, count, top, most, lean):
    order = jax.random.permutation(stream_key, count)
    heavy_load, common = shares(count, rows * top, most, lean, True), shares(count, rows * top, most, lean, False)
    places = jnp.arange(count)

    def named(lengths, offset_by):
        used = int((lengths > 0).sum())
        fixed = max(1, used // 4)
        moved = fixed + (places - fixed + offset_by * (used - fixed)) % max(1, count - fixed)
        return jnp.zeros((count,), jnp.int32).at[order[jnp.where(places < fixed, places, moved)]].set(jnp.asarray(lengths, jnp.int32))

    lengths = jnp.where(number % 4 == 0, named(heavy_load, number // 4), named(common, number - number // 4 - 1))
    mixed = jax.random.permutation(jax.random.fold_in(own, 3), count)
    donor, sink = mixed[0:count // 2 * 2:2], mixed[1:count // 2 * 2:2]
    slack = jnp.minimum(lengths[donor] - 1, most - lengths[sink]) // 2
    slack = jnp.where((donor == order[0]) | (sink == order[0]) | (lengths[sink] == 0), 0, jnp.maximum(slack, 0))
    moved = jax.random.randint(jax.random.fold_in(own, 4), (count // 2,), 0, 1 << 20) % (slack + 1)
    lengths = lengths.at[donor].add(-moved).at[sink].add(moved)
    items = jnp.searchsorted(jnp.cumsum(lengths), jnp.arange(rows * top), side="right").astype(jnp.int32)
    listing = items.reshape(top, rows).T
    listing = listing[jax.random.permutation(jax.random.fold_in(own, 1), rows)]
    offset_by = jax.random.randint(jax.random.fold_in(own, 2), (rows, 1), 0, top)
    return jnp.take_along_axis(listing, (jnp.arange(top)[None, :] + offset_by) % top, axis=1)


def shares(count, total, reach, lean, full):
    weights = [(1 << 20) // math.isqrt(grade ** lean) + 1 for grade in range(1, count + 1)]
    largest = reach if full else min(reach, max(-(-total // count), total * weights[0] // sum(weights)))
    least = 1 if total - largest >= count - 1 else 0
    counts, surplus = [largest] + [least] * (count - 1), total - largest - least * (count - 1)
    while surplus > 0:
        free = [i for i in range(1, count) if counts[i] < largest] or [i for i in range(1, count) if counts[i] < reach]
        mass, remaining = sum([weights[i] for i in free]), surplus
        for i in free:
            addition = min(reach - counts[i], max(1, remaining * weights[i] // mass), surplus)
            counts[i] = counts[i] + addition
            surplus = surplus - addition
    return np.array(counts)


def noise(rng, shape, deviation, bound, pieces=(), held_as=jnp.bfloat16):
    gain = block_scale(rng, shape, pieces, -0.22, 0.18) if pieces else 1.0
    entries = jax.random.normal(rng, shape, jnp.float32) * deviation * gain
    return jnp.minimum(jnp.maximum(entries, -bound), bound).astype(held_as)


def setup_inputs(seed: int = 0, part: int = 0) -> dict:
    key_list = jax.random.split(jax.random.key(seed), 6)
    own_keys = jax.random.split(jax.random.fold_in(key_list[5], part), 6)
    tiles = noise(own_keys[0], (NTILES, TILE, TILE), 0.07, 0.41992188, ((0, 16),))
    tile_row_keys = jax.random.split(jax.random.fold_in(own_keys[1], 1), NTILES // NT_DEV)
    tile_row_turns = jax.random.permutation(jax.random.fold_in(own_keys[1], 3), NTILES // NT_DEV)
    tile_row = jax.vmap(lambda own, number: deal_out(jax.random.fold_in(own_keys[1], 2), own, number, NT_DEV, NB, 1, CAP, 2))(tile_row_keys, tile_row_turns).reshape((NTILES, 1))
    tile_col_keys = jax.random.split(jax.random.fold_in(own_keys[2], 1), NTILES // NT_DEV)
    tile_col_turns = jax.random.permutation(jax.random.fold_in(own_keys[2], 3), NTILES // NT_DEV)
    tile_col = jax.vmap(lambda own, number: deal_out(jax.random.fold_in(own_keys[2], 2), own, number, NT_DEV, NB, 1, CAP, 2))(tile_col_keys, tile_col_turns).reshape((NTILES, 1))
    tile_aux = place_ends(jax.random.randint(own_keys[3], (NTILES,), 0, AUX), jax.random.fold_in(own_keys[3], 1), 0, AUX - 1).astype(jnp.int32)
    coeffs = noise(own_keys[4], (NBF, NOCC), TILE ** -0.5, 0.5, ((0, 16),))
    return {"tiles": tiles, "tile_row": tile_row, "tile_col": tile_col, "tile_aux": tile_aux, "coeffs": coeffs}


def reference(tiles, tile_row, tile_col, tile_aux, coeffs):
    blocks = coeffs.reshape(NBF // TILE, TILE, NOCC)
    batch = blocks[:, :, :OI]
    group = 128
    count = tiles.shape[0] // group
    rows_all = tile_row[:, 0]
    cols_all = tile_col[:, 0]

    def step(total, index):
        start = (index * group).astype(jnp.int32)
        piece = lax.dynamic_slice_in_dim(tiles, start, group, 0)
        rows = lax.dynamic_slice_in_dim(rows_all, start, group, 0)
        cols = lax.dynamic_slice_in_dim(cols_all, start, group, 0)
        auxes = lax.dynamic_slice_in_dim(tile_aux, start, group, 0)
        lefts = jnp.einsum("snq,snm->sqm", batch[rows].astype(jnp.float32), piece.astype(jnp.float32)).astype(jnp.bfloat16)
        contrib = jnp.einsum("sqm,smj->sqj", lefts.astype(jnp.float32), blocks[cols].astype(jnp.float32))
        return total.at[auxes].add(contrib), None

    total, unused = lax.scan(step, jnp.zeros((AUX, OI, NOCC), jnp.float32), jnp.arange(count, dtype=jnp.int32))
    return total
```

```python
import functools
import jax
import jax.numpy as jnp
from jax import lax
from jax.experimental import pallas as pl
from jax.experimental.pallas import tpu as pltpu
from jax.sharding import PartitionSpec as P

OI = 96
AUX = 16
CAP = 2
MESH = pl.DeviceIdType.MESH
VMEM = pl.BlockSpec(memory_space=pltpu.VMEM)
SMEM = pl.BlockSpec(memory_space=pltpu.SMEM)
ANY = pl.BlockSpec(memory_space=pl.ANY)
LIMIT = 48 * 1024 * 1024


def greet(peers):
    barrier = pltpu.get_barrier_semaphore()
    for peer in peers:
        pl.semaphore_signal(barrier, inc=1, device_id={"row": peer}, device_id_type=MESH)
    pl.semaphore_wait(barrier, len(peers))


def remote(src, dst, send, recv, peer):
    return pltpu.make_async_remote_copy(
        src_ref=src, dst_ref=dst, send_sem=send, recv_sem=recv,
        device_id={"row": peer}, device_id_type=MESH,
    )


def gather_kernel(devices, own_ref, all_ref, zs, zr, ys, yr, cs, cr):
    me = lax.axis_index("row")
    blk = own_ref.shape[0]
    depth = devices // 4
    z, y, core = me // 4, (me // 2) % 2, me % 2

    def index(zz, yy, cc):
        return (zz * 2 + yy) * 2 + cc

    def at(dev):
        return all_ref.at[pl.ds(dev * blk, blk)]

    z_peers = [index((z + i) % depth, y, core) for i in range(1, depth)]
    over_y, over_core = index(z, 1 - y, core), index(z, y, 1 - core)
    greet(z_peers + [over_y, over_core])
    all_ref[pl.ds(me * blk, blk)] = own_ref[...]
    copies = []
    z_copies = []
    for i, peer in enumerate(z_peers):
        copy = remote(own_ref, at(me), zs.at[i], zr.at[i], peer)
        copy.start()
        z_copies.append(copy)
    y_copies, c_copies = [], []

    def forward_y(i, dev):
        src = own_ref if i == 0 else at(dev)
        copy = remote(src, at(dev), ys.at[i], yr.at[i], over_y)
        copy.start()
        y_copies.append(copy)

    def forward_core(i, dev):
        src = own_ref if i == 0 else at(dev)
        copy = remote(src, at(dev), cs.at[i], cr.at[i], over_core)
        copy.start()
        c_copies.append(copy)

    forward_y(0, me)
    forward_core(0, me)
    for i in range(1, depth):
        z_copies[i - 1].wait_recv()
        dev = index((z + depth - i) % depth, y, core)
        forward_y(i, dev)
        forward_core(i, dev)
    for i in range(depth):
        y_copies[i].wait_recv()
        forward_core(depth + i, index((z + depth - i) % depth, 1 - y, core))
    for copy in c_copies:
        copy.wait_recv()
    for copy in z_copies + y_copies + c_copies:
        copy.wait_send()


def gather(own, devices):
    depth = devices // 4
    dma = pltpu.SemaphoreType.DMA
    return pl.pallas_call(
        functools.partial(gather_kernel, devices),
        out_shape=jax.ShapeDtypeStruct((devices * own.shape[0],) + own.shape[1:], own.dtype),
        in_specs=[VMEM],
        out_specs=VMEM,
        scratch_shapes=[dma((depth,))] * 4 + [dma((2 * depth,))] * 2,
        compiler_params=pltpu.CompilerParams(
            collective_id=0, has_side_effects=True, vmem_limit_bytes=LIMIT
        ),
    )(own)


def left_kernel(row_ref, col_ref, aux_ref, batch_ref, tiles_ref, packed_ref, marks_ref, seen_ref):
    count = tiles_ref.shape[0]
    slots = marks_ref.shape[0]
    marks_ref[...] = jnp.full(marks_ref.shape, AUX, jnp.int32)

    def clear(b, carry):
        seen_ref[b] = 0
        return carry

    lax.fori_loop(0, slots // CAP, clear, 0)
    width = 8

    def step(g, carry):
        lefts = []
        for u in range(width):
            t = g * width + u
            lefts.append(
                jnp.dot(
                    batch_ref[row_ref[t, 0]], tiles_ref[t], preferred_element_type=jnp.float32
                ).astype(jnp.bfloat16)
            )
        for u in range(width):
            t = g * width + u
            c = col_ref[t, 0]
            rank = seen_ref[c]
            seen_ref[c] = rank + 1
            slot = c * CAP + rank
            packed_ref[slot] = lefts[u]
            marks_ref[slot] = jnp.full((1, 128), aux_ref[t], jnp.int32)
        return carry

    lax.fori_loop(0, count // width, step, 0)


def lefts(tile_row, tile_col, tile_aux, batch, tiles):
    slots = batch.shape[0] * CAP
    tile = tiles.shape[1]
    return pl.pallas_call(
        left_kernel,
        out_shape=[
            jax.ShapeDtypeStruct((slots, OI, tile), jnp.bfloat16),
            jax.ShapeDtypeStruct((slots, 1, 128), jnp.int32),
        ],
        in_specs=[SMEM, SMEM, SMEM, VMEM, VMEM],
        out_specs=[VMEM, VMEM],
        scratch_shapes=[pltpu.SMEM((batch.shape[0],), jnp.int32)],
        compiler_params=pltpu.CompilerParams(vmem_limit_bytes=LIMIT),
    )(tile_row, tile_col, tile_aux, batch, tiles)


def exchange_kernel(devices, x_ref, m_ref, x_out, m_out, own, xs, xr, ms, mr):
    me = lax.axis_index("row")
    per = x_ref.shape[0] // devices

    def part(ref, dev):
        return ref.at[pl.ds(dev * per, per)]

    peers = [(me + i) % devices for i in range(1, devices)]
    greet(peers)
    copies = []
    for i, peer in enumerate(peers):
        copies.append(remote(part(m_ref, peer), part(m_out, me), ms.at[i], mr.at[i], peer))
        copies.append(remote(part(x_ref, peer), part(x_out, me), xs.at[i], xr.at[i], peer))
    for copy in copies:
        copy.start()
    mine = [
        pltpu.make_async_copy(part(x_ref, me), part(x_out, me), own.at[0]),
        pltpu.make_async_copy(part(m_ref, me), part(m_out, me), own.at[1]),
    ]
    for copy in mine:
        copy.start()
    for copy in mine:
        copy.wait()
    for copy in copies:
        copy.wait_recv()
    for copy in copies:
        copy.wait_send()


def exchange(x, marks, devices):
    dma = pltpu.SemaphoreType.DMA
    return pl.pallas_call(
        functools.partial(exchange_kernel, devices),
        out_shape=[
            jax.ShapeDtypeStruct(x.shape, x.dtype),
            jax.ShapeDtypeStruct(marks.shape, marks.dtype),
        ],
        in_specs=[ANY, ANY],
        out_specs=[ANY, ANY],
        scratch_shapes=[dma((2,))] + [dma((devices,))] * 4,
        compiler_params=pltpu.CompilerParams(collective_id=1, has_side_effects=True),
    )(x, marks)


def place_kernel(devices, aux_ref, got_ref, coeffs_ref, out_ref, sums, dense):
    blk = sums.shape[0]
    sums[...] = jnp.zeros_like(sums)

    def add(p, carry):
        for b in range(blk):
            for r in range(CAP):
                s = (p * blk + b) * CAP + r
                a = aux_ref[s]
                sums[b, a] += got_ref[s].astype(jnp.float32)
        return carry

    lax.fori_loop(0, devices, add, 0)
    tile = got_ref.shape[2]
    for b in range(blk):
        for a in range(AUX):
            dense[pl.ds(a * OI, OI), pl.ds(b * tile, tile)] = sums[b, a].astype(jnp.bfloat16)
    width = out_ref.shape[2]
    chips = devices // 2

    def column(n, carry):
        turned = coeffs_ref[n]
        whole = lax.dot_general(
            turned, dense[...], (((1,), (1,)), ((), ())), preferred_element_type=jnp.float32
        ).astype(jnp.bfloat16)
        out_ref[0, n] = whole[:width]
        out_ref[1, n] = whole[width:]
        return carry

    lax.fori_loop(0, chips, column, 0)


def place(aux, got, turned, devices):
    chips, both, depth = turned.shape
    tile = got.shape[2]
    return pl.pallas_call(
        functools.partial(place_kernel, devices),
        out_shape=jax.ShapeDtypeStruct((2, chips, both // 2, AUX * OI), jnp.bfloat16),
        in_specs=[SMEM, VMEM, VMEM],
        out_specs=VMEM,
        scratch_shapes=[
            pltpu.VMEM((depth // tile, AUX + 1, OI, tile), jnp.float32),
            pltpu.VMEM((AUX * OI, depth), jnp.bfloat16),
        ],
        compiler_params=pltpu.CompilerParams(vmem_limit_bytes=LIMIT),
    )(aux, got, turned)


def reduce_kernel(devices, part_ref, out_ref, near, held, far, a_s, a_r, b_s, b_r):
    me = lax.axis_index("row")
    chips = devices // 2
    chip, core = me // 2, me % 2
    partner = chip * 2 + 1 - core
    peers = [((chip + i) % chips) * 2 + core for i in range(1, chips)]
    greet(peers + [partner])
    first = []
    for i in range(1, chips + 1):
        n = (chip + i) % chips
        copy = remote(part_ref.at[1 - core, n], near.at[n], a_s.at[i - 1], a_r.at[i - 1], partner)
        copy.start()
        first.append(copy)
    second = []
    for i in range(1, chips):
        n = (chip + i) % chips
        first[i - 1].wait_recv()
        held[n] = (
            part_ref[core, n].astype(jnp.float32) + near[n].astype(jnp.float32)
        ).astype(jnp.bfloat16)
        copy = remote(held.at[n], far.at[chip], b_s.at[i - 1], b_r.at[i - 1], peers[i - 1])
        copy.start()
        second.append(copy)
    first[chips - 1].wait_recv()
    out_ref[...] = part_ref[core, chip].astype(jnp.float32) + near[chip].astype(jnp.float32)
    for i in range(1, chips):
        second[i - 1].wait_recv()
        out_ref[...] += far[(chip + chips - i) % chips].astype(jnp.float32)
    for copy in first + second:
        copy.wait_send()


def reduce(part, devices):
    chips = devices // 2
    block = part.shape[2:]
    dma = pltpu.SemaphoreType.DMA
    slots = pltpu.VMEM((chips,) + block, jnp.bfloat16)
    return pl.pallas_call(
        functools.partial(reduce_kernel, devices),
        out_shape=jax.ShapeDtypeStruct(block, jnp.float32),
        in_specs=[VMEM],
        out_specs=VMEM,
        scratch_shapes=[slots] * 3 + [dma((chips,))] * 4,
        compiler_params=pltpu.CompilerParams(
            collective_id=2, has_side_effects=True, vmem_limit_bytes=LIMIT
        ),
    )(part)


def on_device(devices, tiles, tile_row, tile_col, tile_aux, coeffs):
    tile = tiles.shape[1]
    rows, occupied = coeffs.shape
    chips = devices // 2
    own = coeffs[:, :OI].reshape(rows // tile, tile, OI).transpose(0, 2, 1)
    turned = coeffs.T.reshape(chips, occupied // chips, rows)
    batch = gather(own, devices)
    packed, marks = lefts(tile_row, tile_col, tile_aux, batch, tiles)
    got, got_marks = exchange(packed, marks, devices)
    part = place(got_marks[:, 0, 0], got, turned, devices)
    total = reduce(part, devices)
    return total.T.reshape(AUX, OI, occupied // devices)


def solution(mesh):
    placed = (
        P(("groups", "row"), None, None),
        P(("groups", "row"), None),
        P(("groups", "row"), None),
        P(("groups", "row")),
        P(("groups", "row"), None),
    )
    return jax.shard_map(
        functools.partial(on_device, mesh.shape["row"]),
        mesh=mesh, in_specs=placed, out_specs=P("groups", None, "row"), check_vma=False,
    )
```

```python
import functools
import jax
import jax.numpy as jnp
from jax import lax
from jax.experimental import pallas as pl
from jax.experimental.pallas import tpu as pltpu
from jax.sharding import PartitionSpec as P

OI = 96
AUX = 16
CAP = 2
MESH = pl.DeviceIdType.MESH
VMEM = pl.BlockSpec(memory_space=pltpu.VMEM)
SMEM = pl.BlockSpec(memory_space=pltpu.SMEM)
ANY = pl.BlockSpec(memory_space=pl.ANY)
LIMIT = 48 * 1024 * 1024


def greet(peers):
    barrier = pltpu.get_barrier_semaphore()
    for peer in peers:
        pl.semaphore_signal(barrier, inc=1, device_id={"row": peer}, device_id_type=MESH)
    pl.semaphore_wait(barrier, len(peers))


def remote(src, dst, send, recv, peer):
    return pltpu.make_async_remote_copy(
        src_ref=src, dst_ref=dst, send_sem=send, recv_sem=recv,
        device_id={"row": peer}, device_id_type=MESH,
    )


def gather_kernel(devices, own_ref, all_ref, zs, zr, ys, yr, cs, cr):
    me = lax.axis_index("row")
    blk = own_ref.shape[0]
    depth = devices // 4
    z, y, core = me // 4, (me // 2) % 2, me % 2

    def index(zz, yy, cc):
        return (zz * 2 + yy) * 2 + cc

    def at(dev):
        return all_ref.at[pl.ds(dev * blk, blk)]

    z_peers = [index((z + i) % depth, y, core) for i in range(1, depth)]
    over_y, over_core = index(z, 1 - y, core), index(z, y, 1 - core)
    greet(z_peers + [over_y, over_core])
    all_ref[pl.ds(me * blk, blk)] = own_ref[...]
    copies = []
    z_copies = []
    for i, peer in enumerate(z_peers):
        copy = remote(own_ref, at(me), zs.at[i], zr.at[i], peer)
        copy.start()
        z_copies.append(copy)
    y_copies, c_copies = [], []

    def forward_y(i, dev):
        src = own_ref if i == 0 else at(dev)
        copy = remote(src, at(dev), ys.at[i], yr.at[i], over_y)
        copy.start()
        y_copies.append(copy)

    def forward_core(i, dev):
        src = own_ref if i == 0 else at(dev)
        copy = remote(src, at(dev), cs.at[i], cr.at[i], over_core)
        copy.start()
        c_copies.append(copy)

    forward_y(0, me)
    forward_core(0, me)
    for i in range(1, depth):
        z_copies[i - 1].wait_recv()
        dev = index((z + depth - i) % depth, y, core)
        forward_y(i, dev)
        forward_core(i, dev)
    for i in range(depth):
        y_copies[i].wait_recv()
        forward_core(depth + i, index((z + depth - i) % depth, 1 - y, core))
    for copy in c_copies:
        copy.wait_recv()
    for copy in z_copies + y_copies + c_copies:
        copy.wait_send()


def gather(own, devices):
    depth = devices // 4
    dma = pltpu.SemaphoreType.DMA
    return pl.pallas_call(
        functools.partial(gather_kernel, devices),
        out_shape=jax.ShapeDtypeStruct((devices * own.shape[0],) + own.shape[1:], own.dtype),
        in_specs=[VMEM],
        out_specs=VMEM,
        scratch_shapes=[dma((depth,))] * 4 + [dma((2 * depth,))] * 2,
        compiler_params=pltpu.CompilerParams(
            collective_id=0, has_side_effects=True, vmem_limit_bytes=LIMIT
        ),
    )(own)


def left_kernel(devices, row_ref, col_ref, aux_ref, batch_ref, tiles_ref, packed_ref, marks_ref, seen_ref):
    count = tiles_ref.shape[0]
    blocks = batch_ref.shape[0]
    half = devices // 2
    blk = blocks // devices
    per = 2 * blk * CAP

    def clear(b, carry):
        seen_ref[b] = 0
        for r in range(CAP):
            s = b * CAP + r
            marks_ref[lax.div(s, per), 0, lax.rem(s, per)] = AUX
        return carry

    lax.fori_loop(0, blocks, clear, 0)
    width = 8

    def step(g, carry):
        lefts = []
        for u in range(width):
            t = g * width + u
            lefts.append(
                jnp.dot(
                    batch_ref[row_ref[t, 0]], tiles_ref[t], preferred_element_type=jnp.float32
                ).astype(jnp.bfloat16)
            )
        for u in range(width):
            t = g * width + u
            c = col_ref[t, 0]
            rank = seen_ref[c]
            seen_ref[c] = rank + 1
            dev = lax.div(c, blk)
            dest = lax.rem(dev, half)
            at = (lax.div(dev, half) * blk + lax.rem(c, blk)) * CAP + rank
            packed_ref[dest * per + at] = lefts[u]
            marks_ref[dest, 0, at] = aux_ref[t]
        return carry

    lax.fori_loop(0, count // width, step, 0)


def lefts(tile_row, tile_col, tile_aux, batch, tiles, devices):
    slots = batch.shape[0] * CAP
    tile = tiles.shape[1]
    return pl.pallas_call(
        functools.partial(left_kernel, devices),
        out_shape=[
            jax.ShapeDtypeStruct((slots, OI, tile), jnp.bfloat16),
            jax.ShapeDtypeStruct((devices // 2, 1, 128), jnp.int32),
        ],
        in_specs=[SMEM, SMEM, SMEM, VMEM, VMEM],
        out_specs=[VMEM, SMEM],
        scratch_shapes=[pltpu.SMEM((batch.shape[0],), jnp.int32)],
        compiler_params=pltpu.CompilerParams(vmem_limit_bytes=LIMIT),
    )(tile_row, tile_col, tile_aux, batch, tiles)


def exchange_kernel(devices, x_ref, m_ref, x_out, m_out, own, xs, xr, ms, mr):
    me = lax.axis_index("row")
    half = devices // 2
    base, place_at = (me // half) * half, me % half
    per = x_ref.shape[0] // half

    def part(ref, j):
        return ref.at[pl.ds(j * per, per)]

    others = [(place_at + i) % half for i in range(1, half)]
    greet([base + j for j in others])
    copies = []
    for i, j in enumerate(others):
        copies.append(remote(m_ref.at[j], m_out.at[place_at], ms.at[i], mr.at[i], base + j))
        copies.append(
            remote(part(x_ref, j), part(x_out, place_at), xs.at[i], xr.at[i], base + j)
        )
    for copy in copies:
        copy.start()
    mine = [
        pltpu.make_async_copy(part(x_ref, place_at), part(x_out, place_at), own.at[0]),
        pltpu.make_async_copy(m_ref.at[place_at], m_out.at[place_at], own.at[1]),
    ]
    for copy in mine:
        copy.start()
    for copy in mine:
        copy.wait()
    for copy in copies:
        copy.wait_recv()
    for copy in copies:
        copy.wait_send()


def exchange(x, marks, devices):
    dma = pltpu.SemaphoreType.DMA
    return pl.pallas_call(
        functools.partial(exchange_kernel, devices),
        out_shape=[
            jax.ShapeDtypeStruct(x.shape, x.dtype),
            jax.ShapeDtypeStruct(marks.shape, marks.dtype),
        ],
        in_specs=[ANY, ANY],
        out_specs=[ANY, ANY],
        scratch_shapes=[dma((2,))] + [dma((devices // 2,))] * 4,
        compiler_params=pltpu.CompilerParams(collective_id=1, has_side_effects=True),
    )(x, marks)


def place_kernel(devices, aux_ref, got_ref, dense_ref, sums):
    half = devices // 2
    blk = sums.shape[1]
    tile = got_ref.shape[2]
    side = lax.div(lax.axis_index("row"), half)
    sums[...] = jnp.zeros_like(sums)

    def add(p, carry):
        for h in range(2):
            local = (side if h == 0 else 1 - side) * blk * CAP
            for b in range(blk):
                for r in range(CAP):
                    k = local + b * CAP + r
                    a = aux_ref[p, 0, k]
                    sums[h, b, a] += got_ref[p * 2 * blk * CAP + k].astype(jnp.float32)
        return carry

    lax.fori_loop(0, half, add, 0)
    for h in range(2):
        for b in range(blk):
            for a in range(AUX):
                dense_ref[h, pl.ds(a * OI, OI), pl.ds(b * tile, tile)] = sums[h, b, a].astype(
                    jnp.bfloat16
                )


def place(aux, got, devices, blk):
    tile = got.shape[2]
    return pl.pallas_call(
        functools.partial(place_kernel, devices),
        out_shape=jax.ShapeDtypeStruct((2, AUX * OI, blk * tile), jnp.bfloat16),
        in_specs=[SMEM, VMEM],
        out_specs=VMEM,
        scratch_shapes=[pltpu.VMEM((2, blk, AUX + 1, OI, tile), jnp.float32)],
        compiler_params=pltpu.CompilerParams(vmem_limit_bytes=LIMIT),
    )(aux, got)


def reduce_kernel(
    devices, dense_ref, here_ref, there_ref, out_ref,
    parts, near, held_y, far_y, held_z, far_z, a_s, a_r, b_s, b_r, c_s, c_r,
):
    me = lax.axis_index("row")
    depth = devices // 4
    rows = out_ref.shape[0]
    z, y, core = me // 4, (me // 2) % 2, me % 2
    f32, bf16 = jnp.float32, jnp.bfloat16

    def index(zz, yy, cc):
        return (zz * 2 + yy) * 2 + cc

    over_y, over_core = index(z, 1 - y, core), index(z, y, 1 - core)
    to = [(z + i) % depth for i in range(1, depth)] + [z]
    z_peers = [index(zz, y, core) for zz in to[:-1]]
    greet(z_peers + [over_y, over_core])
    turn = (((1,), (1,)), ((), ()))
    a_copies, b_copies, c_copies = [], [], []

    def to_y(i):
        zz = to[i]
        a_copies[2 * i].wait_recv()
        held_y[zz] = (
            parts[zz, 1 - y, core].astype(f32) + near[zz, 1 - y].astype(f32)
        ).astype(bf16)
        copy = remote(held_y.at[zz], far_y.at[zz], b_s.at[i], b_r.at[i], over_y)
        copy.start()
        b_copies.append(copy)

    for i, zz in enumerate(to):
        whole = lax.dot_general(here_ref[zz], dense_ref[0], turn, preferred_element_type=f32)
        whole += lax.dot_general(there_ref[zz], dense_ref[1], turn, preferred_element_type=f32)
        parts[zz] = whole.astype(bf16).reshape(2, 2, rows, whole.shape[1])
        for k, yy in enumerate((1 - y, y)):
            copy = remote(
                parts.at[zz, yy, 1 - core], near.at[zz, yy],
                a_s.at[2 * i + k], a_r.at[2 * i + k], over_core,
            )
            copy.start()
            a_copies.append(copy)
        if i:
            to_y(i - 1)
    to_y(depth - 1)
    for i, zz in enumerate(to):
        a_copies[2 * i + 1].wait_recv()
        b_copies[i].wait_recv()
        total = (
            parts[zz, y, core].astype(f32) + near[zz, y].astype(f32) + far_y[zz].astype(f32)
        )
        if i == depth - 1:
            out_ref[...] = total
        else:
            held_z[zz] = total.astype(bf16)
            copy = remote(held_z.at[zz], far_z.at[z], c_s.at[i], c_r.at[i], z_peers[i])
            copy.start()
            c_copies.append(copy)
    for i in range(1, depth):
        c_copies[i - 1].wait_recv()
        out_ref[...] += far_z[(z + depth - i) % depth].astype(f32)
    for copy in a_copies + b_copies + c_copies:
        copy.wait_send()


def reduce(dense, here, there, devices):
    depth = devices // 4
    rows = here.shape[1] // 4
    wide = dense.shape[1]
    dma = pltpu.SemaphoreType.DMA

    def slots(*lead):
        return pltpu.VMEM(lead + (rows, wide), jnp.bfloat16)

    return pl.pallas_call(
        functools.partial(reduce_kernel, devices),
        out_shape=jax.ShapeDtypeStruct((rows, wide), jnp.float32),
        in_specs=[VMEM] * 3,
        out_specs=VMEM,
        scratch_shapes=[slots(depth, 2, 2), slots(depth, 2)]
        + [slots(depth)] * 4
        + [dma((2 * depth,))] * 2
        + [dma((depth,))] * 4,
        compiler_params=pltpu.CompilerParams(
            collective_id=2, has_side_effects=True, vmem_limit_bytes=LIMIT
        ),
    )(dense, here, there)


def on_device(devices, tiles, tile_row, tile_col, tile_aux, coeffs):
    tile = tiles.shape[1]
    rows, occupied = coeffs.shape
    half, depth = devices // 2, devices // 4
    here = coeffs.T.reshape(depth, occupied // depth, rows)
    there = lax.ppermute(here, "row", [(i, (i + half) % devices) for i in range(devices)])
    own = coeffs[:, :OI].reshape(rows // tile, tile, OI).transpose(0, 2, 1)
    batch = gather(own, devices)
    packed, marks = lefts(tile_row, tile_col, tile_aux, batch, tiles, devices)
    got, got_marks = exchange(packed, marks, devices)
    dense = place(got_marks, got, devices, rows // tile)
    total = reduce(dense, here, there, devices)
    return total.T.reshape(AUX, OI, occupied // devices)


def solution(mesh):
    placed = (
        P(("groups", "row"), None, None),
        P(("groups", "row"), None),
        P(("groups", "row"), None),
        P(("groups", "row")),
        P(("groups", "row"), None),
    )
    return jax.shard_map(
        functools.partial(on_device, mesh.shape["row"]),
        mesh=mesh, in_specs=placed, out_specs=P("groups", None, "row"), check_vma=False,
    )
```

```python
import functools
import jax
import jax.numpy as jnp
from jax import lax
from jax.experimental import pallas as pl
from jax.experimental.pallas import tpu as pltpu
from jax.sharding import PartitionSpec as P

OI = 96
AUX = 16
CAP = 2
MESH = pl.DeviceIdType.MESH
VMEM = pl.BlockSpec(memory_space=pltpu.VMEM)
SMEM = pl.BlockSpec(memory_space=pltpu.SMEM)
ANY = pl.BlockSpec(memory_space=pl.ANY)
LIMIT = 48 * 1024 * 1024


def greet(peers):
    barrier = pltpu.get_barrier_semaphore()
    for peer in peers:
        pl.semaphore_signal(barrier, inc=1, device_id={"row": peer}, device_id_type=MESH)
    pl.semaphore_wait(barrier, len(peers))


def remote(src, dst, send, recv, peer):
    return pltpu.make_async_remote_copy(
        src_ref=src, dst_ref=dst, send_sem=send, recv_sem=recv,
        device_id={"row": peer}, device_id_type=MESH,
    )


def gather_kernel(devices, own_ref, all_ref, zs, zr, ys, yr, cs, cr):
    me = lax.axis_index("row")
    blk = own_ref.shape[0]
    depth = devices // 4
    z, y, core = me // 4, (me // 2) % 2, me % 2

    def index(zz, yy, cc):
        return (zz * 2 + yy) * 2 + cc

    def at(dev):
        return all_ref.at[pl.ds(dev * blk, blk)]

    z_peers = [index((z + i) % depth, y, core) for i in range(1, depth)]
    over_y, over_core = index(z, 1 - y, core), index(z, y, 1 - core)
    greet(z_peers + [over_y, over_core])
    all_ref[pl.ds(me * blk, blk)] = own_ref[...]
    copies = []
    z_copies = []
    for i, peer in enumerate(z_peers):
        copy = remote(own_ref, at(me), zs.at[i], zr.at[i], peer)
        copy.start()
        z_copies.append(copy)
    y_copies, c_copies = [], []

    def forward_y(i, dev):
        src = own_ref if i == 0 else at(dev)
        copy = remote(src, at(dev), ys.at[i], yr.at[i], over_y)
        copy.start()
        y_copies.append(copy)

    def forward_core(i, dev):
        src = own_ref if i == 0 else at(dev)
        copy = remote(src, at(dev), cs.at[i], cr.at[i], over_core)
        copy.start()
        c_copies.append(copy)

    forward_y(0, me)
    forward_core(0, me)
    for i in range(1, depth):
        z_copies[i - 1].wait_recv()
        dev = index((z + depth - i) % depth, y, core)
        forward_y(i, dev)
        forward_core(i, dev)
    for i in range(depth):
        y_copies[i].wait_recv()
        forward_core(depth + i, index((z + depth - i) % depth, 1 - y, core))
    for copy in c_copies:
        copy.wait_recv()
    for copy in z_copies + y_copies + c_copies:
        copy.wait_send()


def gather(own, devices):
    depth = devices // 4
    dma = pltpu.SemaphoreType.DMA
    return pl.pallas_call(
        functools.partial(gather_kernel, devices),
        out_shape=jax.ShapeDtypeStruct((devices * own.shape[0],) + own.shape[1:], own.dtype),
        in_specs=[VMEM],
        out_specs=VMEM,
        scratch_shapes=[dma((depth,))] * 4 + [dma((2 * depth,))] * 2,
        compiler_params=pltpu.CompilerParams(
            collective_id=0, has_side_effects=True, vmem_limit_bytes=LIMIT
        ),
    )(own)


def left_kernel(devices, row_ref, col_ref, aux_ref, batch_ref, tiles_ref, packed_ref, marks_ref, seen_ref):
    count = tiles_ref.shape[0]
    blocks = batch_ref.shape[0]
    half = devices // 2
    blk = blocks // devices
    per = 2 * blk * CAP

    def clear(b, carry):
        seen_ref[b] = 0
        for r in range(CAP):
            s = b * CAP + r
            marks_ref[lax.div(s, per), 0, lax.rem(s, per)] = AUX
        return carry

    lax.fori_loop(0, blocks, clear, 0)
    width = 8

    def step(g, carry):
        lefts = []
        for u in range(width):
            t = g * width + u
            lefts.append(
                jnp.dot(
                    batch_ref[row_ref[t, 0]], tiles_ref[t], preferred_element_type=jnp.float32
                ).astype(jnp.bfloat16)
            )
        for u in range(width):
            t = g * width + u
            c = col_ref[t, 0]
            rank = seen_ref[c]
            seen_ref[c] = rank + 1
            dev = lax.div(c, blk)
            dest = lax.rem(dev, half)
            at = (lax.div(dev, half) * blk + lax.rem(c, blk)) * CAP + rank
            packed_ref[dest * per + at] = lefts[u]
            marks_ref[dest, 0, at] = aux_ref[t]
        return carry

    lax.fori_loop(0, count // width, step, 0)


def lefts(tile_row, tile_col, tile_aux, batch, tiles, devices):
    slots = batch.shape[0] * CAP
    tile = tiles.shape[1]
    return pl.pallas_call(
        functools.partial(left_kernel, devices),
        out_shape=[
            jax.ShapeDtypeStruct((slots, OI, tile), jnp.bfloat16),
            jax.ShapeDtypeStruct((devices // 2, 1, 128), jnp.int32),
        ],
        in_specs=[SMEM, SMEM, SMEM, VMEM, VMEM],
        out_specs=[VMEM, SMEM],
        scratch_shapes=[pltpu.SMEM((batch.shape[0],), jnp.int32)],
        compiler_params=pltpu.CompilerParams(vmem_limit_bytes=LIMIT),
    )(tile_row, tile_col, tile_aux, batch, tiles)


def exchange_kernel(devices, x_ref, m_ref, x_out, m_out, own, xs, xr, ms, mr):
    me = lax.axis_index("row")
    half = devices // 2
    base, place_at = (me // half) * half, me % half
    per = x_ref.shape[0] // half

    def part(ref, j):
        return ref.at[pl.ds(j * per, per)]

    others = [(place_at + i) % half for i in range(1, half)]
    greet([base + j for j in others])
    copies = []
    for i, j in enumerate(others):
        copies.append(remote(m_ref.at[j], m_out.at[place_at], ms.at[i], mr.at[i], base + j))
        copies.append(
            remote(part(x_ref, j), part(x_out, place_at), xs.at[i], xr.at[i], base + j)
        )
    for copy in copies:
        copy.start()
    mine = [
        pltpu.make_async_copy(part(x_ref, place_at), part(x_out, place_at), own.at[0]),
        pltpu.make_async_copy(m_ref.at[place_at], m_out.at[place_at], own.at[1]),
    ]
    for copy in mine:
        copy.start()
    for copy in mine:
        copy.wait()
    for copy in copies:
        copy.wait_recv()
    for copy in copies:
        copy.wait_send()


def exchange(x, marks, devices):
    dma = pltpu.SemaphoreType.DMA
    return pl.pallas_call(
        functools.partial(exchange_kernel, devices),
        out_shape=[
            jax.ShapeDtypeStruct(x.shape, x.dtype),
            jax.ShapeDtypeStruct(marks.shape, marks.dtype),
        ],
        in_specs=[ANY, ANY],
        out_specs=[ANY, ANY],
        scratch_shapes=[dma((2,))] + [dma((devices // 2,))] * 4,
        compiler_params=pltpu.CompilerParams(collective_id=1, has_side_effects=True),
    )(x, marks)


def place_kernel(devices, aux_ref, got_ref, dense_ref, sums):
    half = devices // 2
    blk = sums.shape[1]
    tile = got_ref.shape[2]
    side = lax.div(lax.axis_index("row"), half)
    sums[...] = jnp.zeros_like(sums)

    def add(p, carry):
        for h in range(2):
            local = (side if h == 0 else 1 - side) * blk * CAP
            for b in range(blk):
                for r in range(CAP):
                    k = local + b * CAP + r
                    a = aux_ref[p, 0, k]
                    sums[h, b, a] += got_ref[p * 2 * blk * CAP + k].astype(jnp.float32)
        return carry

    lax.fori_loop(0, half, add, 0)
    for h in range(2):
        for b in range(blk):
            for a in range(AUX):
                dense_ref[h, pl.ds(a * OI, OI), pl.ds(b * tile, tile)] = sums[h, b, a].astype(
                    jnp.bfloat16
                )


def place(aux, got, devices, blk):
    tile = got.shape[2]
    return pl.pallas_call(
        functools.partial(place_kernel, devices),
        out_shape=jax.ShapeDtypeStruct((2, AUX * OI, blk * tile), jnp.bfloat16),
        in_specs=[SMEM, VMEM],
        out_specs=VMEM,
        scratch_shapes=[pltpu.VMEM((2, blk, AUX + 1, OI, tile), jnp.float32)],
        compiler_params=pltpu.CompilerParams(vmem_limit_bytes=LIMIT),
    )(aux, got)


def reduce_kernel(
    devices, dense_ref, here_ref, there_ref, out_ref,
    parts, near, held_y, far_y, held_z, far_z, a_s, a_r, b_s, b_r, c_s, c_r,
):
    me = lax.axis_index("row")
    depth = devices // 4
    rows = out_ref.shape[0]
    z, y, core = me // 4, (me // 2) % 2, me % 2
    f32, bf16 = jnp.float32, jnp.bfloat16

    def index(zz, yy, cc):
        return (zz * 2 + yy) * 2 + cc

    over_y, over_core = index(z, 1 - y, core), index(z, y, 1 - core)
    to = [(z + i) % depth for i in range(1, depth)] + [z]
    z_peers = [index(zz, y, core) for zz in to[:-1]]
    greet(z_peers + [over_y, over_core])
    turn = (((1,), (1,)), ((), ()))
    a_copies, b_copies, c_copies = [], [], []

    def to_y(i):
        zz = to[i]
        a_copies[2 * i].wait_recv()
        held_y[zz] = (
            parts[zz, 1 - y, core].astype(f32) + near[zz, 1 - y].astype(f32)
        ).astype(bf16)
        copy = remote(held_y.at[zz], far_y.at[zz], b_s.at[i], b_r.at[i], over_y)
        copy.start()
        b_copies.append(copy)

    for i, zz in enumerate(to):
        whole = lax.dot_general(here_ref[zz], dense_ref[0], turn, preferred_element_type=f32)
        whole += lax.dot_general(there_ref[zz], dense_ref[1], turn, preferred_element_type=f32)
        parts[zz] = whole.astype(bf16).reshape(2, 2, rows, whole.shape[1])
        for k, yy in enumerate((1 - y, y)):
            copy = remote(
                parts.at[zz, yy, 1 - core], near.at[zz, yy],
                a_s.at[2 * i + k], a_r.at[2 * i + k], over_core,
            )
            copy.start()
            a_copies.append(copy)
        if i:
            to_y(i - 1)
    to_y(depth - 1)
    for i, zz in enumerate(to):
        a_copies[2 * i + 1].wait_recv()
        b_copies[i].wait_recv()
        total = (
            parts[zz, y, core].astype(f32) + near[zz, y].astype(f32) + far_y[zz].astype(f32)
        )
        if i == depth - 1:
            out_ref[...] = total
        else:
            held_z[zz] = total.astype(bf16)
            copy = remote(held_z.at[zz], far_z.at[z], c_s.at[i], c_r.at[i], z_peers[i])
            copy.start()
            c_copies.append(copy)
    for i in range(1, depth):
        c_copies[i - 1].wait_recv()
        out_ref[...] += far_z[(z + depth - i) % depth].astype(f32)
    for copy in a_copies + b_copies + c_copies:
        copy.wait_send()


def reduce(dense, here, there, devices):
    depth = devices // 4
    rows = here.shape[1] // 4
    wide = dense.shape[1]
    dma = pltpu.SemaphoreType.DMA

    def slots(*lead):
        return pltpu.VMEM(lead + (rows, wide), jnp.bfloat16)

    return pl.pallas_call(
        functools.partial(reduce_kernel, devices),
        out_shape=jax.ShapeDtypeStruct((rows, wide), jnp.float32),
        in_specs=[VMEM] * 3,
        out_specs=VMEM,
        scratch_shapes=[slots(depth, 2, 2), slots(depth, 2)]
        + [slots(depth)] * 4
        + [dma((2 * depth,))] * 2
        + [dma((depth,))] * 4,
        compiler_params=pltpu.CompilerParams(
            collective_id=2, has_side_effects=True, vmem_limit_bytes=LIMIT
        ),
    )(dense, here, there)


def on_device(devices, tiles, tile_row, tile_col, tile_aux, coeffs):
    tile = tiles.shape[1]
    rows, occupied = coeffs.shape
    half, depth = devices // 2, devices // 4
    here = coeffs.T.reshape(depth, occupied // depth, rows)
    own = coeffs[:, :OI].reshape(rows // tile, tile, OI).transpose(0, 2, 1)
    batch = gather(own, devices)
    here, batch = lax.optimization_barrier((here, batch))
    there = lax.ppermute(here, "row", [(i, (i + half) % devices) for i in range(devices)])
    packed, marks = lefts(tile_row, tile_col, tile_aux, batch, tiles, devices)
    got, got_marks = exchange(packed, marks, devices)
    dense = place(got_marks, got, devices, rows // tile)
    total = reduce(dense, here, there, devices)
    return total.T.reshape(AUX, OI, occupied // devices)


def solution(mesh):
    placed = (
        P(("groups", "row"), None, None),
        P(("groups", "row"), None),
        P(("groups", "row"), None),
        P(("groups", "row")),
        P(("groups", "row"), None),
    )
    return jax.shard_map(
        functools.partial(on_device, mesh.shape["row"]),
        mesh=mesh, in_specs=placed, out_specs=P("groups", None, "row"), check_vma=False,
    )
```

```python
import functools
import jax
import jax.numpy as jnp
from jax import lax
from jax.experimental import pallas as pl
from jax.experimental.pallas import tpu as pltpu
from jax.sharding import PartitionSpec as P

OI = 96
AUX = 16
CAP = 2
MESH = pl.DeviceIdType.MESH
VMEM = pl.BlockSpec(memory_space=pltpu.VMEM)
SMEM = pl.BlockSpec(memory_space=pltpu.SMEM)
ANY = pl.BlockSpec(memory_space=pl.ANY)
LIMIT = 48 * 1024 * 1024


def greet(peers):
    barrier = pltpu.get_barrier_semaphore()
    for peer in peers:
        pl.semaphore_signal(barrier, inc=1, device_id={"row": peer}, device_id_type=MESH)
    pl.semaphore_wait(barrier, len(peers))


def remote(src, dst, send, recv, peer):
    return pltpu.make_async_remote_copy(
        src_ref=src, dst_ref=dst, send_sem=send, recv_sem=recv,
        device_id={"row": peer}, device_id_type=MESH,
    )


def slots_kernel(devices, blk, col_ref, aux_ref, pick_ref, marks_ref, seen_ref):
    half = devices // 2
    per = 2 * blk * CAP
    for b in range(devices * blk):
        seen_ref[b] = 0
    for j in range(half):
        for k in range(per):
            marks_ref[j, 0, k] = AUX
            pick_ref[j * per + k] = 0

    def step(t, carry):
        c = col_ref[t]
        rank = seen_ref[c]
        seen_ref[c] = rank + 1
        dev = lax.div(c, blk)
        dest = lax.rem(dev, half)
        at = (lax.div(dev, half) * blk + lax.rem(c, blk)) * CAP + rank
        pick_ref[dest * per + at] = t
        marks_ref[dest, 0, at] = aux_ref[t]
        return carry

    lax.fori_loop(0, col_ref.shape[0], step, 0, unroll=4)


def choose_slots(tile_col, tile_aux, devices, blk):
    blocks = devices * blk
    return pl.pallas_call(
        functools.partial(slots_kernel, devices, blk),
        out_shape=[
            jax.ShapeDtypeStruct((blocks * CAP,), jnp.int32),
            jax.ShapeDtypeStruct((devices // 2, 1, 128), jnp.int32),
        ],
        in_specs=[SMEM, SMEM],
        out_specs=[SMEM, SMEM],
        scratch_shapes=[pltpu.SMEM((blocks,), jnp.int32)],
    )(tile_col, tile_aux)


def build_kernel(
    devices, row_ref, pick_ref, own_ref, tiles_ref, here_ref, m_ref,
    got_ref, m_out, there_ref,
    batch_ref, send_ref, zs, zr, ys, yr, cs, cr, hs, hr, xs, xr, ms, mr, local,
):
    me = lax.axis_index("row")
    blk = own_ref.shape[0]
    depth, half = devices // 4, devices // 2
    deep = depth // 2
    z, y, core = me // 4, (me // 2) % 2, me % 2
    side, place_at = me // half, me % half
    per = 2 * blk * CAP

    def index(zz, yy, cc):
        return (zz * 2 + yy) * 2 + cc

    def at(dev):
        return batch_ref.at[pl.ds(dev * blk, blk)]

    def part(ref, j):
        return ref.at[pl.ds(j * per, per)]

    z_peers = [index((z + i) % depth, y, core) for i in range(1, depth)]
    over_y, over_core = index(z, 1 - y, core), index(z, y, 1 - core)
    across = (me + half) % devices
    relative = [(dz, a, b) for dz in range(1, deep) for a in range(2) for b in range(2)]
    relative += [(0, 1, 0), (0, 1, 1), (0, 0, 1)]
    targets = [
        index((z % deep + dz) % deep, (y + a) % 2, (core + b) % 2) for dz, a, b in relative
    ]
    greet(
        [side * half + j for j in targets]
        + [index((1 - side) * deep + k, y, core) for k in range(deep)]
    )
    z_copies, y_copies, c_copies, h_copies, x_copies = [], [], [], [], []
    for i, peer in enumerate(z_peers):
        copy = remote(own_ref, at(me), zs.at[i], zr.at[i], peer)
        copy.start()
        z_copies.append(copy)

    def forward(copies, i, dev, send, recv, peer):
        src = own_ref if i == 0 else at(dev)
        copy = remote(src, at(dev), send.at[i], recv.at[i], peer)
        copy.start()
        copies.append(copy)

    forward(y_copies, 0, me, ys, yr, over_y)
    forward(c_copies, 0, me, cs, cr, over_core)
    for i in range(depth):
        copy = remote(here_ref.at[i], there_ref.at[i], hs.at[i], hr.at[i], across)
        copy.start()
        h_copies.append(copy)
    batch_ref[pl.ds(me * blk, blk)] = own_ref[...]
    for i in range(1, depth):
        z_copies[i - 1].wait_recv()
        dev = index((z + depth - i) % depth, y, core)
        forward(y_copies, i, dev, ys, yr, over_y)
        forward(c_copies, i, dev, cs, cr, over_core)
    for i in range(depth):
        y_copies[i].wait_recv()
        dev = index((z + depth - i) % depth, 1 - y, core)
        forward(c_copies, depth + i, dev, cs, cr, over_core)
    for copy in c_copies:
        copy.wait_recv()

    width = min(8, per)

    def fill(ref, j):
        def step(g, carry):
            first = j * per + g * width
            for u in range(width):
                t = pick_ref[first + u]
                ref[first + u] = jnp.dot(
                    batch_ref[row_ref[t]], tiles_ref[t], preferred_element_type=jnp.float32
                ).astype(jnp.bfloat16)
            return carry

        lax.fori_loop(0, per // width, step, 0)

    for i, j in enumerate(targets):
        peer = side * half + j
        fill(send_ref, j)
        x_copies.append(
            remote(part(send_ref, j), part(got_ref, place_at), xs.at[i], xr.at[i], peer)
        )
        x_copies.append(remote(m_ref.at[j], m_out.at[place_at], ms.at[i], mr.at[i], peer))
        x_copies[-2].start()
        x_copies[-1].start()
    mine = pltpu.make_async_copy(m_ref.at[place_at], m_out.at[place_at], local.at[0])
    mine.start()
    fill(got_ref, place_at)
    mine.wait()
    for copy in x_copies + h_copies:
        copy.wait_recv()
    for copy in z_copies + y_copies + c_copies + h_copies + x_copies:
        copy.wait_send()


def build(tile_row, pick, own, tiles, here, marks, devices):
    depth, half = devices // 4, devices // 2
    dma = pltpu.SemaphoreType.DMA
    tile = tiles.shape[1]
    slots = pick.shape[0]
    return pl.pallas_call(
        functools.partial(build_kernel, devices),
        out_shape=[
            jax.ShapeDtypeStruct((slots, OI, tile), jnp.bfloat16),
            jax.ShapeDtypeStruct(marks.shape, marks.dtype),
            jax.ShapeDtypeStruct(here.shape, here.dtype),
        ],
        in_specs=[SMEM, SMEM, VMEM, VMEM, VMEM, ANY],
        out_specs=[VMEM, ANY, VMEM],
        scratch_shapes=[
            pltpu.VMEM((devices * own.shape[0],) + own.shape[1:], own.dtype),
            pltpu.VMEM((slots, OI, tile), jnp.bfloat16),
        ]
        + [dma((depth,))] * 4
        + [dma((2 * depth,))] * 2
        + [dma((depth,))] * 2
        + [dma((half,))] * 4
        + [dma((1,))],
        compiler_params=pltpu.CompilerParams(
            collective_id=0, has_side_effects=True, vmem_limit_bytes=LIMIT
        ),
    )(tile_row, pick, own, tiles, here, marks)


def place_kernel(devices, aux_ref, got_ref, dense_ref, sums):
    half = devices // 2
    blk = sums.shape[1]
    tile = got_ref.shape[2]
    side = lax.div(lax.axis_index("row"), half)
    sums[...] = jnp.zeros_like(sums)

    def add(p, carry):
        for h in range(2):
            local = (side if h == 0 else 1 - side) * blk * CAP
            for b in range(blk):
                for r in range(CAP):
                    k = local + b * CAP + r
                    a = aux_ref[p, 0, k]
                    sums[h, b, a] += got_ref[p * 2 * blk * CAP + k].astype(jnp.float32)
        return carry

    lax.fori_loop(0, half, add, 0)
    for h in range(2):
        for b in range(blk):
            for a in range(AUX):
                dense_ref[h, pl.ds(a * OI, OI), pl.ds(b * tile, tile)] = sums[h, b, a].astype(
                    jnp.bfloat16
                )


def place(aux, got, devices, blk):
    tile = got.shape[2]
    return pl.pallas_call(
        functools.partial(place_kernel, devices),
        out_shape=jax.ShapeDtypeStruct((2, AUX * OI, blk * tile), jnp.bfloat16),
        in_specs=[SMEM, VMEM],
        out_specs=VMEM,
        scratch_shapes=[pltpu.VMEM((2, blk, AUX + 1, OI, tile), jnp.float32)],
        compiler_params=pltpu.CompilerParams(vmem_limit_bytes=LIMIT),
    )(aux, got)


def reduce_kernel(
    devices, dense_ref, here_ref, there_ref, out_ref,
    parts, near, held_y, far_y, held_z, far_z, a_s, a_r, b_s, b_r, c_s, c_r,
):
    me = lax.axis_index("row")
    depth = devices // 4
    rows = out_ref.shape[0]
    z, y, core = me // 4, (me // 2) % 2, me % 2
    f32, bf16 = jnp.float32, jnp.bfloat16

    def index(zz, yy, cc):
        return (zz * 2 + yy) * 2 + cc

    over_y, over_core = index(z, 1 - y, core), index(z, y, 1 - core)
    to = [(z + i) % depth for i in range(1, depth)] + [z]
    z_peers = [index(zz, y, core) for zz in to[:-1]]
    greet(z_peers + [over_y, over_core])
    turn = (((1,), (1,)), ((), ()))
    a_copies, b_copies, c_copies = [], [], []

    def to_y(i):
        zz = to[i]
        a_copies[2 * i].wait_recv()
        held_y[zz] = (
            parts[zz, 1 - y, core].astype(f32) + near[zz, 1 - y].astype(f32)
        ).astype(bf16)
        copy = remote(held_y.at[zz], far_y.at[zz], b_s.at[i], b_r.at[i], over_y)
        copy.start()
        b_copies.append(copy)

    for i, zz in enumerate(to):
        whole = lax.dot_general(here_ref[zz], dense_ref[0], turn, preferred_element_type=f32)
        whole += lax.dot_general(there_ref[zz], dense_ref[1], turn, preferred_element_type=f32)
        parts[zz] = whole.astype(bf16).reshape(2, 2, rows, whole.shape[1])
        for k, yy in enumerate((1 - y, y)):
            copy = remote(
                parts.at[zz, yy, 1 - core], near.at[zz, yy],
                a_s.at[2 * i + k], a_r.at[2 * i + k], over_core,
            )
            copy.start()
            a_copies.append(copy)
        if i:
            to_y(i - 1)
    to_y(depth - 1)
    for i, zz in enumerate(to):
        a_copies[2 * i + 1].wait_recv()
        b_copies[i].wait_recv()
        total = (
            parts[zz, y, core].astype(f32) + near[zz, y].astype(f32) + far_y[zz].astype(f32)
        )
        if i == depth - 1:
            out_ref[...] = total
        else:
            held_z[zz] = total.astype(bf16)
            copy = remote(held_z.at[zz], far_z.at[z], c_s.at[i], c_r.at[i], z_peers[i])
            copy.start()
            c_copies.append(copy)
    for i in range(1, depth):
        c_copies[i - 1].wait_recv()
        out_ref[...] += far_z[(z + depth - i) % depth].astype(f32)
    for copy in a_copies + b_copies + c_copies:
        copy.wait_send()


def reduce(dense, here, there, devices):
    depth = devices // 4
    rows = here.shape[1] // 4
    wide = dense.shape[1]
    dma = pltpu.SemaphoreType.DMA

    def slots(*lead):
        return pltpu.VMEM(lead + (rows, wide), jnp.bfloat16)

    return pl.pallas_call(
        functools.partial(reduce_kernel, devices),
        out_shape=jax.ShapeDtypeStruct((rows, wide), jnp.float32),
        in_specs=[VMEM] * 3,
        out_specs=VMEM,
        scratch_shapes=[slots(depth, 2, 2), slots(depth, 2)]
        + [slots(depth)] * 4
        + [dma((2 * depth,))] * 2
        + [dma((depth,))] * 4,
        compiler_params=pltpu.CompilerParams(
            collective_id=1, has_side_effects=True, vmem_limit_bytes=LIMIT
        ),
    )(dense, here, there)


def on_device(devices, tiles, tile_row, tile_col, tile_aux, coeffs):
    tile = tiles.shape[1]
    rows, occupied = coeffs.shape
    blk, depth = rows // tile, devices // 4
    here = coeffs.T.reshape(depth, occupied // depth, rows)
    own = coeffs[:, :OI].reshape(blk, tile, OI).transpose(0, 2, 1)
    pick, marks = choose_slots(tile_col.reshape(-1), tile_aux, devices, blk)
    got, got_marks, there = build(tile_row.reshape(-1), pick, own, tiles, here, marks, devices)
    dense = place(got_marks, got, devices, blk)
    total = reduce(dense, here, there, devices)
    return total.T.reshape(AUX, OI, occupied // devices)


def solution(mesh):
    placed = (
        P(("groups", "row"), None, None),
        P(("groups", "row"), None),
        P(("groups", "row"), None),
        P(("groups", "row")),
        P(("groups", "row"), None),
    )
    return jax.shard_map(
        functools.partial(on_device, mesh.shape["row"]),
        mesh=mesh, in_specs=placed, out_specs=P("groups", None, "row"), check_vma=False,
    )
```

```python
import functools
import jax
import jax.numpy as jnp
from jax import lax
from jax.experimental import pallas as pl
from jax.experimental.pallas import tpu as pltpu
from jax.sharding import PartitionSpec as P

OI = 96
AUX = 16
CAP = 2
MESH = pl.DeviceIdType.MESH
VMEM = pl.BlockSpec(memory_space=pltpu.VMEM)
SMEM = pl.BlockSpec(memory_space=pltpu.SMEM)
ANY = pl.BlockSpec(memory_space=pl.ANY)
EARLY = 1
LIMIT = 48 * 1024 * 1024


def greet(peers):
    barrier = pltpu.get_barrier_semaphore()
    for peer in peers:
        pl.semaphore_signal(barrier, inc=1, device_id={"row": peer}, device_id_type=MESH)
    pl.semaphore_wait(barrier, len(peers))


def remote(src, dst, send, recv, peer):
    return pltpu.make_async_remote_copy(
        src_ref=src, dst_ref=dst, send_sem=send, recv_sem=recv,
        device_id={"row": peer}, device_id_type=MESH,
    )


def log2(size):
    return size.bit_length() - 1


def choose_slots(devices, blk, row_ref, col_ref, aux_ref):
    count = col_ref.shape[1]
    half = devices // 2
    per = 2 * blk * CAP
    slots = half * per
    down = lax.broadcasted_iota(jnp.int32, (count, count), 0)
    right = lax.broadcasted_iota(jnp.int32, (count, count), 1)

    def upright(ref):
        return jnp.sum(jnp.where(down == right, ref[...], 0), axis=1, keepdims=True)

    rows, cols, auxes = upright(row_ref), upright(col_ref), upright(aux_ref)
    earlier = jnp.logical_and(cols == col_ref[...], right < down)
    rank = jnp.sum(jnp.where(earlier, 1, 0), axis=1, keepdims=True)
    dev = lax.shift_right_logical(cols, jnp.full_like(cols, log2(blk)))
    dest = dev & (half - 1)
    upper = lax.shift_right_logical(dev, jnp.full_like(dev, log2(half)))
    slot = dest * per + (upper * blk + (cols & (blk - 1))) * CAP + rank
    hit = slot == lax.broadcasted_iota(jnp.int32, (count, slots), 1)
    which = lax.broadcasted_iota(jnp.int32, (count, slots), 0)

    def chosen(values):
        return jnp.sum(jnp.where(hit, values, 0), axis=0, keepdims=True)

    return chosen(which), chosen(rows), chosen(auxes - AUX) + AUX


def build_kernel(
    devices, row_ref, col_ref, aux_ref, coeffs_ref, tiles_hbm,
    got_ref, m_out, here_ref, there_ref,
    own_ref, tiles_ref, slot_ref, m_ref, pick_ref, at_row_ref,
    batch_ref, send_ref, zs, zr, ys, yr, cs, cr, hs, hr, xs, xr, ms, mr, local,
):
    me = lax.axis_index("row")
    blk = own_ref.shape[0]
    depth, half = devices // 4, devices // 2
    deep = depth // 2
    z, y, core = me // 4, (me // 2) % 2, me % 2
    side, place_at = me // half, me % half
    per = 2 * blk * CAP

    def index(zz, yy, cc):
        return (zz * 2 + yy) * 2 + cc

    def at(dev):
        return batch_ref.at[pl.ds(dev * blk, blk)]

    def part(ref, j):
        return ref.at[pl.ds(j * per, per)]

    z_peers = [index((z + i) % depth, y, core) for i in range(1, depth)]
    over_y, over_core = index(z, 1 - y, core), index(z, y, 1 - core)
    across = (me + half) % devices
    relative = [(dz, a, b) for dz in range(1, deep) for a in range(2) for b in range(2)]
    relative += [(0, 1, 0), (0, 1, 1), (0, 0, 1)]
    targets = [
        index((z % deep + dz) % deep, (y + a) % 2, (core + b) % 2) for dz, a, b in relative
    ]
    tile = own_ref.shape[2]
    for b in range(blk):
        own_ref[b] = coeffs_ref[pl.ds(b * tile, tile), pl.ds(0, 128)].T[:OI]
    greet(
        [side * half + j for j in targets]
        + [index((1 - side) * deep + k, y, core) for k in range(deep)]
    )
    load = pltpu.make_async_copy(tiles_hbm, tiles_ref, local.at[0])
    load.start()
    z_copies, y_copies, c_copies, h_copies, x_copies = [], [], [], [], []
    for i, peer in enumerate(z_peers):
        copy = remote(own_ref, at(me), zs.at[i], zr.at[i], peer)
        copy.start()
        z_copies.append(copy)

    def forward(copies, i, dev, send, recv, peer):
        src = own_ref if i == 0 else at(dev)
        copy = remote(src, at(dev), send.at[i], recv.at[i], peer)
        copy.start()
        copies.append(copy)

    forward(y_copies, 0, me, ys, yr, over_y)
    forward(c_copies, 0, me, cs, cr, over_core)

    wide = here_ref.shape[0] // depth

    def swap(i):
        piece = pl.ds(i * wide, wide)
        copy = remote(here_ref.at[piece], there_ref.at[piece], hs.at[i], hr.at[i], across)
        copy.start()
        h_copies.append(copy)

    batch_ref[pl.ds(me * blk, blk)] = own_ref[...]
    picks, rows_of, marks = choose_slots(devices, blk, row_ref, col_ref, aux_ref)
    slot_ref[0] = picks
    slot_ref[1] = rows_of
    m_ref[...] = marks
    moves = [
        pltpu.make_async_copy(slot_ref.at[0], pick_ref, local.at[1]),
        pltpu.make_async_copy(slot_ref.at[1], at_row_ref, local.at[2]),
    ]
    for move in moves:
        move.start()
    for n in range(here_ref.shape[0] // 128):
        here_ref[pl.ds(n * 128, 128), :] = coeffs_ref[:, pl.ds(n * 128, 128)].T
    for i in range(1, depth):
        z_copies[i - 1].wait_recv()
        dev = index((z + depth - i) % depth, y, core)
        forward(y_copies, i, dev, ys, yr, over_y)
        forward(c_copies, i, dev, cs, cr, over_core)
    for i in range(depth):
        y_copies[i].wait_recv()
        dev = index((z + depth - i) % depth, 1 - y, core)
        forward(c_copies, depth + i, dev, cs, cr, over_core)
    for i in range(EARLY):
        swap(i)
    for copy in c_copies:
        copy.wait_recv()

    load.wait()
    for move in moves:
        move.wait()
    width = min(8, per)

    def fill(ref, j):
        def step(g, carry):
            first = j * per + g * width
            for u in range(width):
                left = batch_ref[at_row_ref[0, first + u]]
                ref[first + u] = jnp.dot(
                    left, tiles_ref[pick_ref[0, first + u]], preferred_element_type=jnp.float32
                ).astype(jnp.bfloat16)
            return carry

        lax.fori_loop(0, per // width, step, 0)

    for i, j in enumerate(targets):
        peer = side * half + j
        fill(send_ref, j)
        x_copies.append(
            remote(part(send_ref, j), part(got_ref, place_at), xs.at[i], xr.at[i], peer)
        )
        x_copies.append(remote(m_ref, m_out.at[place_at], ms.at[i], mr.at[i], peer))
        x_copies[-2].start()
        x_copies[-1].start()
        if len(h_copies) < depth:
            swap(len(h_copies))
    m_out[place_at] = m_ref[...]
    fill(got_ref, place_at)
    for copy in x_copies + h_copies:
        copy.wait_recv()
    for copy in z_copies + y_copies + c_copies + h_copies + x_copies:
        copy.wait_send()


def build(tile_row, tile_col, tile_aux, coeffs, tiles, devices):
    depth, half = devices // 4, devices // 2
    dma = pltpu.SemaphoreType.DMA
    count, tile = tiles.shape[:2]
    rows, occupied = coeffs.shape
    blk = rows // tile
    slots = devices * blk * CAP
    turned = jax.ShapeDtypeStruct((occupied, rows), coeffs.dtype)
    return pl.pallas_call(
        functools.partial(build_kernel, devices),
        out_shape=[
            jax.ShapeDtypeStruct((slots, OI, tile), jnp.bfloat16),
            jax.ShapeDtypeStruct((half, 1, slots), jnp.int32),
            turned,
            turned,
        ],
        in_specs=[VMEM, VMEM, VMEM, VMEM, ANY],
        out_specs=[VMEM] * 4,
        scratch_shapes=[
            pltpu.VMEM((blk, OI, tile), coeffs.dtype),
            pltpu.VMEM(tiles.shape, tiles.dtype),
            pltpu.VMEM((2, 1, slots), jnp.int32),
            pltpu.VMEM((1, slots), jnp.int32),
            pltpu.SMEM((1, slots), jnp.int32),
            pltpu.SMEM((1, slots), jnp.int32),
            pltpu.VMEM((devices * blk, OI, tile), coeffs.dtype),
            pltpu.VMEM((slots, OI, tile), jnp.bfloat16),
        ]
        + [dma((depth,))] * 4
        + [dma((2 * depth,))] * 2
        + [dma((depth,))] * 2
        + [dma((half,))] * 4
        + [dma((3,))],
        compiler_params=pltpu.CompilerParams(
            collective_id=0, has_side_effects=True, vmem_limit_bytes=LIMIT
        ),
    )(tile_row, tile_col, tile_aux, coeffs, tiles)


def place_kernel(devices, aux_ref, got_ref, dense_ref, sums):
    half = devices // 2
    blk = sums.shape[1]
    tile = got_ref.shape[2]
    side = lax.div(lax.axis_index("row"), half)
    start = lax.rem(lax.axis_index("row"), half) * 2 * blk * CAP
    sums[...] = jnp.zeros_like(sums)

    def add(p, carry):
        for h in range(2):
            local = (side if h == 0 else 1 - side) * blk * CAP
            for b in range(blk):
                for r in range(CAP):
                    k = local + b * CAP + r
                    a = aux_ref[p, 0, start + k]
                    sums[h, b, a] += got_ref[p * 2 * blk * CAP + k].astype(jnp.float32)
        return carry

    lax.fori_loop(0, half, add, 0)
    for h in range(2):
        for b in range(blk):
            for a in range(AUX):
                dense_ref[h, pl.ds(a * OI, OI), pl.ds(b * tile, tile)] = sums[h, b, a].astype(
                    jnp.bfloat16
                )


def place(aux, got, devices, blk):
    tile = got.shape[2]
    return pl.pallas_call(
        functools.partial(place_kernel, devices),
        out_shape=jax.ShapeDtypeStruct((2, AUX * OI, blk * tile), jnp.bfloat16),
        in_specs=[SMEM, VMEM],
        out_specs=VMEM,
        scratch_shapes=[pltpu.VMEM((2, blk, AUX + 1, OI, tile), jnp.float32)],
        compiler_params=pltpu.CompilerParams(vmem_limit_bytes=LIMIT),
    )(aux, got)


def reduce_kernel(
    devices, dense_ref, here_ref, there_ref, out_ref,
    parts, near, held_y, far_y, held_z, far_z, a_s, a_r, b_s, b_r, c_s, c_r,
):
    me = lax.axis_index("row")
    depth = devices // 4
    rows = out_ref.shape[0]
    z, y, core = me // 4, (me // 2) % 2, me % 2
    f32, bf16 = jnp.float32, jnp.bfloat16

    def index(zz, yy, cc):
        return (zz * 2 + yy) * 2 + cc

    over_y, over_core = index(z, 1 - y, core), index(z, y, 1 - core)
    to = [(z + i) % depth for i in range(1, depth)] + [z]
    z_peers = [index(zz, y, core) for zz in to[:-1]]
    greet(z_peers + [over_y, over_core])
    turn = (((1,), (1,)), ((), ()))
    a_copies, b_copies, c_copies = [], [], []

    def to_y(i):
        zz = to[i]
        a_copies[2 * i].wait_recv()
        held_y[zz] = (
            parts[zz, 1 - y, core].astype(f32) + near[zz, 1 - y].astype(f32)
        ).astype(bf16)
        copy = remote(held_y.at[zz], far_y.at[zz], b_s.at[i], b_r.at[i], over_y)
        copy.start()
        b_copies.append(copy)

    for i, zz in enumerate(to):
        piece = pl.ds(zz * 4 * rows, 4 * rows)
        whole = lax.dot_general(
            here_ref[piece, :], dense_ref[0], turn, preferred_element_type=f32
        )
        whole += lax.dot_general(
            there_ref[piece, :], dense_ref[1], turn, preferred_element_type=f32
        )
        parts[zz] = whole.astype(bf16).reshape(2, 2, rows, whole.shape[1])
        for k, yy in enumerate((1 - y, y)):
            copy = remote(
                parts.at[zz, yy, 1 - core], near.at[zz, yy],
                a_s.at[2 * i + k], a_r.at[2 * i + k], over_core,
            )
            copy.start()
            a_copies.append(copy)
        if i:
            to_y(i - 1)
    to_y(depth - 1)
    for i, zz in enumerate(to):
        a_copies[2 * i + 1].wait_recv()
        b_copies[i].wait_recv()
        total = (
            parts[zz, y, core].astype(f32) + near[zz, y].astype(f32) + far_y[zz].astype(f32)
        )
        if i == depth - 1:
            out_ref[...] = total
        else:
            held_z[zz] = total.astype(bf16)
            copy = remote(held_z.at[zz], far_z.at[z], c_s.at[i], c_r.at[i], z_peers[i])
            copy.start()
            c_copies.append(copy)
    for i in range(1, depth):
        c_copies[i - 1].wait_recv()
        out_ref[...] += far_z[(z + depth - i) % depth].astype(f32)
    for copy in a_copies + b_copies + c_copies:
        copy.wait_send()


def reduce(dense, here, there, devices):
    depth = devices // 4
    rows = here.shape[0] // devices
    wide = dense.shape[1]
    dma = pltpu.SemaphoreType.DMA

    def slots(*lead):
        return pltpu.VMEM(lead + (rows, wide), jnp.bfloat16)

    return pl.pallas_call(
        functools.partial(reduce_kernel, devices),
        out_shape=jax.ShapeDtypeStruct((rows, wide), jnp.float32),
        in_specs=[VMEM] * 3,
        out_specs=VMEM,
        scratch_shapes=[slots(depth, 2, 2), slots(depth, 2)]
        + [slots(depth)] * 4
        + [dma((2 * depth,))] * 2
        + [dma((depth,))] * 4,
        compiler_params=pltpu.CompilerParams(
            collective_id=1, has_side_effects=True, vmem_limit_bytes=LIMIT
        ),
    )(dense, here, there)


def on_device(devices, tiles, tile_row, tile_col, tile_aux, coeffs):
    tile = tiles.shape[1]
    rows, occupied = coeffs.shape
    flat = (1, tiles.shape[0])
    got, got_marks, here, there = build(
        tile_row.reshape(flat), tile_col.reshape(flat), tile_aux.reshape(flat),
        coeffs, tiles, devices,
    )
    dense = place(got_marks, got, devices, rows // tile)
    total = reduce(dense, here, there, devices)
    return total.T.reshape(AUX, OI, occupied // devices)


def solution(mesh):
    placed = (
        P(("groups", "row"), None, None),
        P(("groups", "row"), None),
        P(("groups", "row"), None),
        P(("groups", "row")),
        P(("groups", "row"), None),
    )
    return jax.shard_map(
        functools.partial(on_device, mesh.shape["row"]),
        mesh=mesh, in_specs=placed, out_specs=P("groups", None, "row"), check_vma=False,
    )
```

```python
import functools
import jax
import jax.numpy as jnp
from jax import lax
from jax.experimental import pallas as pl
from jax.experimental.pallas import tpu as pltpu
from jax.sharding import PartitionSpec as P

OI = 96
AUX = 16
CAP = 2
MESH = pl.DeviceIdType.MESH
VMEM = pl.BlockSpec(memory_space=pltpu.VMEM)
SMEM = pl.BlockSpec(memory_space=pltpu.SMEM)
ANY = pl.BlockSpec(memory_space=pl.ANY)
EARLY = 1
LIMIT = 48 * 1024 * 1024
WIDE = 60 * 1024 * 1024


def greet(peers):
    barrier = pltpu.get_barrier_semaphore()
    for peer in peers:
        pl.semaphore_signal(barrier, inc=1, device_id={"row": peer}, device_id_type=MESH)
    pl.semaphore_wait(barrier, len(peers))


def remote(src, dst, send, recv, peer):
    return pltpu.make_async_remote_copy(
        src_ref=src, dst_ref=dst, send_sem=send, recv_sem=recv,
        device_id={"row": peer}, device_id_type=MESH,
    )


def log2(size):
    return size.bit_length() - 1


def choose_slots(devices, blk, row_ref, col_ref, aux_ref):
    count = col_ref.shape[1]
    half = devices // 2
    per = 2 * blk * CAP
    slots = half * per
    down = lax.broadcasted_iota(jnp.int32, (count, count), 0)
    right = lax.broadcasted_iota(jnp.int32, (count, count), 1)

    def upright(ref):
        return jnp.sum(jnp.where(down == right, ref[...], 0), axis=1, keepdims=True)

    rows, cols, auxes = upright(row_ref), upright(col_ref), upright(aux_ref)
    earlier = jnp.logical_and(cols == col_ref[...], right < down)
    rank = jnp.sum(jnp.where(earlier, 1, 0), axis=1, keepdims=True)
    dev = lax.shift_right_logical(cols, jnp.full_like(cols, log2(blk)))
    dest = dev & (half - 1)
    upper = lax.shift_right_logical(dev, jnp.full_like(dev, log2(half)))
    slot = dest * per + (upper * blk + (cols & (blk - 1))) * CAP + rank
    hit = slot == lax.broadcasted_iota(jnp.int32, (count, slots), 1)
    which = lax.broadcasted_iota(jnp.int32, (count, slots), 0)

    def chosen(values):
        return jnp.sum(jnp.where(hit, values, 0), axis=0, keepdims=True)

    return chosen(which), chosen(rows), chosen(auxes - AUX) + AUX


def build_kernel(
    devices, row_ref, col_ref, aux_ref, coeffs_ref, tiles_hbm,
    got_ref, m_out, here_ref, there_ref,
    own_ref, tiles_ref, slot_ref, m_ref, pick_ref, at_row_ref,
    batch_ref, send_ref, zs, zr, ys, yr, cs, cr, hs, hr, xs, xr, ms, mr, local,
):
    me = lax.axis_index("row")
    blk = own_ref.shape[0]
    depth, half = devices // 4, devices // 2
    deep = depth // 2
    z, y, core = me // 4, (me // 2) % 2, me % 2
    side, place_at = me // half, me % half
    per = 2 * blk * CAP

    def index(zz, yy, cc):
        return (zz * 2 + yy) * 2 + cc

    def at(dev):
        return batch_ref.at[pl.ds(dev * blk, blk)]

    def part(ref, j):
        return ref.at[pl.ds(j * per, per)]

    z_peers = [index((z + i) % depth, y, core) for i in range(1, depth)]
    over_y, over_core = index(z, 1 - y, core), index(z, y, 1 - core)
    across = (me + half) % devices
    relative = [(dz, a, b) for dz in range(1, deep) for a in range(2) for b in range(2)]
    relative += [(0, 1, 0), (0, 1, 1), (0, 0, 1)]
    targets = [
        index((z % deep + dz) % deep, (y + a) % 2, (core + b) % 2) for dz, a, b in relative
    ]
    tile = own_ref.shape[2]
    for b in range(blk):
        own_ref[b] = coeffs_ref[pl.ds(b * tile, tile), pl.ds(0, 128)].T[:OI]
    greet(
        [side * half + j for j in targets]
        + [index((1 - side) * deep + k, y, core) for k in range(deep)]
    )
    load = pltpu.make_async_copy(tiles_hbm, tiles_ref, local.at[0])
    load.start()
    z_copies, y_copies, c_copies, h_copies, x_copies = [], [], [], [], []
    for i, peer in enumerate(z_peers):
        copy = remote(own_ref, at(me), zs.at[i], zr.at[i], peer)
        copy.start()
        z_copies.append(copy)

    def forward(copies, i, dev, send, recv, peer):
        src = own_ref if i == 0 else at(dev)
        copy = remote(src, at(dev), send.at[i], recv.at[i], peer)
        copy.start()
        copies.append(copy)

    forward(y_copies, 0, me, ys, yr, over_y)
    forward(c_copies, 0, me, cs, cr, over_core)

    wide = here_ref.shape[0] // depth

    def swap(i):
        piece = pl.ds(i * wide, wide)
        copy = remote(here_ref.at[piece], there_ref.at[piece], hs.at[i], hr.at[i], across)
        copy.start()
        h_copies.append(copy)

    batch_ref[pl.ds(me * blk, blk)] = own_ref[...]
    picks, rows_of, marks = choose_slots(devices, blk, row_ref, col_ref, aux_ref)
    slot_ref[0] = picks
    slot_ref[1] = rows_of
    m_ref[...] = marks
    moves = [
        pltpu.make_async_copy(slot_ref.at[0], pick_ref, local.at[1]),
        pltpu.make_async_copy(slot_ref.at[1], at_row_ref, local.at[2]),
    ]
    for move in moves:
        move.start()
    for n in range(here_ref.shape[0] // 128):
        here_ref[pl.ds(n * 128, 128), :] = coeffs_ref[:, pl.ds(n * 128, 128)].T
    for i in range(1, depth):
        z_copies[i - 1].wait_recv()
        dev = index((z + depth - i) % depth, y, core)
        forward(y_copies, i, dev, ys, yr, over_y)
        forward(c_copies, i, dev, cs, cr, over_core)
    for i in range(depth):
        y_copies[i].wait_recv()
        dev = index((z + depth - i) % depth, 1 - y, core)
        forward(c_copies, depth + i, dev, cs, cr, over_core)
    for i in range(EARLY):
        swap(i)
    for copy in c_copies:
        copy.wait_recv()

    load.wait()
    for move in moves:
        move.wait()
    width = min(8, per)

    def fill(ref, j):
        def step(g, carry):
            first = j * per + g * width
            for u in range(width):
                left = batch_ref[at_row_ref[0, first + u]]
                ref[first + u] = jnp.dot(
                    left, tiles_ref[pick_ref[0, first + u]], preferred_element_type=jnp.float32
                ).astype(jnp.bfloat16)
            return carry

        lax.fori_loop(0, per // width, step, 0)

    for i, j in enumerate(targets):
        peer = side * half + j
        fill(send_ref, j)
        x_copies.append(
            remote(part(send_ref, j), part(got_ref, place_at), xs.at[i], xr.at[i], peer)
        )
        x_copies.append(remote(m_ref, m_out.at[place_at], ms.at[i], mr.at[i], peer))
        x_copies[-2].start()
        x_copies[-1].start()
        if len(h_copies) < depth:
            swap(len(h_copies))
    m_out[place_at] = m_ref[...]
    fill(got_ref, place_at)
    for copy in x_copies + h_copies:
        copy.wait_recv()
    for copy in z_copies + y_copies + c_copies + h_copies + x_copies:
        copy.wait_send()


def build(tile_row, tile_col, tile_aux, coeffs, tiles, devices):
    depth, half = devices // 4, devices // 2
    dma = pltpu.SemaphoreType.DMA
    count, tile = tiles.shape[:2]
    rows, occupied = coeffs.shape
    blk = rows // tile
    slots = devices * blk * CAP
    turned = jax.ShapeDtypeStruct((occupied, rows), coeffs.dtype)
    return pl.pallas_call(
        functools.partial(build_kernel, devices),
        out_shape=[
            jax.ShapeDtypeStruct((slots, OI, tile), jnp.bfloat16),
            jax.ShapeDtypeStruct((half, 1, slots), jnp.int32),
            turned,
            turned,
        ],
        in_specs=[VMEM, VMEM, VMEM, VMEM, ANY],
        out_specs=[VMEM] * 4,
        scratch_shapes=[
            pltpu.VMEM((blk, OI, tile), coeffs.dtype),
            pltpu.VMEM(tiles.shape, tiles.dtype),
            pltpu.VMEM((2, 1, slots), jnp.int32),
            pltpu.VMEM((1, slots), jnp.int32),
            pltpu.SMEM((1, slots), jnp.int32),
            pltpu.SMEM((1, slots), jnp.int32),
            pltpu.VMEM((devices * blk, OI, tile), coeffs.dtype),
            pltpu.VMEM((slots, OI, tile), jnp.bfloat16),
        ]
        + [dma((depth,))] * 4
        + [dma((2 * depth,))] * 2
        + [dma((depth,))] * 2
        + [dma((half,))] * 4
        + [dma((3,))],
        compiler_params=pltpu.CompilerParams(
            collective_id=0, has_side_effects=True, vmem_limit_bytes=WIDE
        ),
    )(tile_row, tile_col, tile_aux, coeffs, tiles)


def place_kernel(devices, aux_ref, got_ref, dense_ref, sums):
    half = devices // 2
    blk = sums.shape[1]
    tile = got_ref.shape[2]
    side = lax.div(lax.axis_index("row"), half)
    start = lax.rem(lax.axis_index("row"), half) * 2 * blk * CAP
    sums[...] = jnp.zeros_like(sums)

    def add(p, carry):
        for h in range(2):
            local = (side if h == 0 else 1 - side) * blk * CAP
            for b in range(blk):
                for r in range(CAP):
                    k = local + b * CAP + r
                    a = aux_ref[p, 0, start + k]
                    sums[h, b, a] += got_ref[p * 2 * blk * CAP + k].astype(jnp.float32)
        return carry

    lax.fori_loop(0, half, add, 0)
    for h in range(2):
        for b in range(blk):
            for a in range(AUX):
                dense_ref[h, pl.ds(a * OI, OI), pl.ds(b * tile, tile)] = sums[h, b, a].astype(
                    jnp.bfloat16
                )


def place(aux, got, devices, blk):
    tile = got.shape[2]
    return pl.pallas_call(
        functools.partial(place_kernel, devices),
        out_shape=jax.ShapeDtypeStruct((2, AUX * OI, blk * tile), jnp.bfloat16),
        in_specs=[SMEM, VMEM],
        out_specs=VMEM,
        scratch_shapes=[pltpu.VMEM((2, blk, AUX + 1, OI, tile), jnp.float32)],
        compiler_params=pltpu.CompilerParams(vmem_limit_bytes=LIMIT),
    )(aux, got)


def reduce_kernel(
    devices, dense_ref, here_ref, there_ref, out_ref,
    parts, near, held_y, far_y, held_z, far_z, a_s, a_r, b_s, b_r, c_s, c_r,
):
    me = lax.axis_index("row")
    depth = devices // 4
    rows = out_ref.shape[0]
    z, y, core = me // 4, (me // 2) % 2, me % 2
    f32, bf16 = jnp.float32, jnp.bfloat16

    def index(zz, yy, cc):
        return (zz * 2 + yy) * 2 + cc

    over_y, over_core = index(z, 1 - y, core), index(z, y, 1 - core)
    to = [(z + i) % depth for i in range(1, depth)] + [z]
    z_peers = [index(zz, y, core) for zz in to[:-1]]
    greet(z_peers + [over_y, over_core])
    turn = (((1,), (1,)), ((), ()))
    a_copies, b_copies, c_copies = [], [], []

    def to_y(i):
        zz = to[i]
        a_copies[2 * i].wait_recv()
        held_y[zz] = (
            parts[zz, 1 - y, core].astype(f32) + near[zz, 1 - y].astype(f32)
        ).astype(bf16)
        copy = remote(held_y.at[zz], far_y.at[zz], b_s.at[i], b_r.at[i], over_y)
        copy.start()
        b_copies.append(copy)

    for i, zz in enumerate(to):
        piece = pl.ds(zz * 4 * rows, 4 * rows)
        whole = lax.dot_general(
            here_ref[piece, :], dense_ref[0], turn, preferred_element_type=f32
        )
        whole += lax.dot_general(
            there_ref[piece, :], dense_ref[1], turn, preferred_element_type=f32
        )
        parts[zz] = whole.astype(bf16).reshape(2, 2, rows, whole.shape[1])
        for k, yy in enumerate((1 - y, y)):
            copy = remote(
                parts.at[zz, yy, 1 - core], near.at[zz, yy],
                a_s.at[2 * i + k], a_r.at[2 * i + k], over_core,
            )
            copy.start()
            a_copies.append(copy)
        if i:
            to_y(i - 1)
    to_y(depth - 1)
    for i, zz in enumerate(to):
        a_copies[2 * i + 1].wait_recv()
        b_copies[i].wait_recv()
        total = (
            parts[zz, y, core].astype(f32) + near[zz, y].astype(f32) + far_y[zz].astype(f32)
        )
        if i == depth - 1:
            out_ref[...] = total
        else:
            held_z[zz] = total.astype(bf16)
            copy = remote(held_z.at[zz], far_z.at[z], c_s.at[i], c_r.at[i], z_peers[i])
            copy.start()
            c_copies.append(copy)
    for i in range(1, depth):
        c_copies[i - 1].wait_recv()
        out_ref[...] += far_z[(z + depth - i) % depth].astype(f32)
    for copy in a_copies + b_copies + c_copies:
        copy.wait_send()


def reduce(dense, here, there, devices):
    depth = devices // 4
    rows = here.shape[0] // devices
    wide = dense.shape[1]
    dma = pltpu.SemaphoreType.DMA

    def slots(*lead):
        return pltpu.VMEM(lead + (rows, wide), jnp.bfloat16)

    return pl.pallas_call(
        functools.partial(reduce_kernel, devices),
        out_shape=jax.ShapeDtypeStruct((rows, wide), jnp.float32),
        in_specs=[VMEM] * 3,
        out_specs=VMEM,
        scratch_shapes=[slots(depth, 2, 2), slots(depth, 2)]
        + [slots(depth)] * 4
        + [dma((2 * depth,))] * 2
        + [dma((depth,))] * 4,
        compiler_params=pltpu.CompilerParams(
            collective_id=1, has_side_effects=True, vmem_limit_bytes=LIMIT
        ),
    )(dense, here, there)


def on_device(devices, tiles, tile_row, tile_col, tile_aux, coeffs):
    tile = tiles.shape[1]
    rows, occupied = coeffs.shape
    flat = (1, tiles.shape[0])
    got, got_marks, here, there = build(
        tile_row.reshape(flat), tile_col.reshape(flat), tile_aux.reshape(flat),
        coeffs, tiles, devices,
    )
    dense = place(got_marks, got, devices, rows // tile)
    total = reduce(dense, here, there, devices)
    return total.T.reshape(AUX, OI, occupied // devices)


def solution(mesh):
    placed = (
        P(("groups", "row"), None, None),
        P(("groups", "row"), None),
        P(("groups", "row"), None),
        P(("groups", "row")),
        P(("groups", "row"), None),
    )
    return jax.shard_map(
        functools.partial(on_device, mesh.shape["row"]),
        mesh=mesh, in_specs=placed, out_specs=P("groups", None, "row"), check_vma=False,
    )
```
